32 devices in a mesh: row: 8 (over z, y), col: 4 (over x, core).
Axes of the slice: x: 2, y: 2, z: 4, core: 2. Of those that a mesh axis runs over, the one named last changes fastest.
Arguments:
- points: float32 [32, 8192], P(None, ('row', 'col')), may hold values from -6 to 6
- candidates: float32 [32, 2048], P(None, ('row', 'col')), may hold values from -6 to 6
- length_scales: float32 [32], replicated, may hold values from 1.5 to 4
- signal_var: float32 [1], replicated, may hold values from 0.5 to 2
- noise_var: float32 [1], replicated, may hold values from 0.1 to 1
- cand_prior: float32 [2048], P(('row', 'col')), may hold values from -6 to 6
- weights: float32 [16, 8192], P(None, ('row', 'col')), may hold values from -6 to 6
- residual: float32 [16, 8192], P(None, ('row', 'col')), may hold values from -300 to 300, as said below
- direction: float32 [16, 8192], P(None, ('row', 'col')), may hold values from -300 to 300, as said below
Outputs:
- weights_new: float32 [16, 8192], P(None, ('row', 'col'))
- residual_new: float32 [16, 8192], P(None, ('row', 'col'))
- direction_new: float32 [16, 8192], P(None, ('row', 'col'))
- cand_fit: float32 [16, 2048], P(None, ('row', 'col'))
The draws below stay inside these ranges and needn't reach their ends.
Inputs may be any that keep to these rules, and one draw needn't show every extreme that they name: `residual`: real values. `direction`: real values.
All inputs are finite; a program needn't handle non-finite values.
Results may differ from the reference program's by a relative error of at most 0.011.
Values may be sent and summed in bfloat16 or wider, within the bound.
A program may use at most 64 MiB of HBM per device.

```python
import math
import jax
import jax.numpy as jnp
from jax import lax

F = 32
COLS = 16
N = 8192
Q = 2048


def rising_field(key, salt):
    key = jax.random.fold_in(key, salt)
    keys = jax.random.split(key, 3)
    positions = jnp.arange(N, dtype=jnp.float32)
    rising = jnp.exp(jnp.log(3.0) * positions / max(N - 1, 1))
    rough = jnp.exp(jnp.log(10.0) * jax.random.uniform(keys[0], (N,), jnp.float32))
    column_scale = jnp.exp(jnp.log(10.0) * jax.random.uniform(keys[1], (COLS, 1), jnp.float32))
    values = jax.random.truncated_normal(keys[2], -5.0, 5.0, (COLS, N), jnp.float32)
    return (values * rising[None, :] * rough[None, :] * column_scale / 10.0).astype(jnp.float32)


def draw_residual(key, part):
    return rising_field(key, 101)


def draw_direction(key, part):
    return rising_field(key, 202)


def steps_of(own_key, extent, shards, smallest, high):
    factor_of, own = 1.0, jax.random.fold_in(own_key, 6)
    for dim, blocks in shards:
        draws = jnp.exp(jax.random.uniform(jax.random.fold_in(own, dim), (blocks,), jnp.float32, smallest / len(shards), high / len(shards)))
        factor_of = factor_of * jnp.repeat(draws, extent[dim] // blocks).reshape([-1 if axis == dim else 1 for axis in range(len(extent))])
    return factor_of


def bell_draw(own_key, extent, spread, reach, cuts=(), kind=jnp.bfloat16):
    array = spread * jax.random.normal(own_key, extent, jnp.float32)
    if cuts:
        array = array * steps_of(own_key, extent, cuts, -0.22, 0.18)
    return jnp.clip(array, -reach, reach).astype(kind)


def setup_inputs(seed: int = 0) -> dict:
    splits = jax.random.split(jax.random.key(seed), 10)
    return {
        "points": bell_draw(splits[0], (F, N), 1.0, 6.0, ((1, 32),), jnp.float32),
        "candidates": bell_draw(splits[1], (F, Q), 1.0, 6.0, ((1, 32),), jnp.float32),
        "length_scales": jnp.clip(jnp.exp(jax.random.uniform(splits[2], (F,), jnp.float32, math.log(1.5), math.log(4.0))), 1.5, 4.0),
        "signal_var": jnp.clip(jnp.exp(jax.random.uniform(splits[3], (1,), jnp.float32, math.log(0.5), math.log(2.0))), 0.5, 2.0),
        "noise_var": jnp.clip(jnp.exp(jax.random.uniform(splits[4], (1,), jnp.float32, math.log(0.1), math.log(1.0))), 0.1, 1.0),
        "cand_prior": bell_draw(splits[5], (Q,), 1.0, 6.0, ((0, 32),), jnp.float32),
        "weights": bell_draw(splits[6], (COLS, N), 1.0, 6.0, ((1, 32),), jnp.float32),
        "residual": draw_residual(jax.random.fold_in(splits[9], 71), 0),
        "direction": draw_direction(jax.random.fold_in(splits[9], 71), 0),
    }


root_five = math.sqrt(5.0)
contract_first = (((0,), (0,)), ((), ()))
contract_last = (((1,), (1,)), ((), ()))

def square_norms(scaled):
    return lax.optimization_barrier(jnp.sum(jnp.square(scaled.astype(jnp.float32)), axis=0))

def matern_block(row_pts, row_sq, col_pts, col_sq, signal_scalar):
    inner_prod = lax.dot_general(row_pts, col_pts, contract_first, preferred_element_type=jnp.float32)
    dist_sq = jnp.maximum(row_sq[:, None] + col_sq[None, :] - 2.0 * inner_prod, 0.0)
    distance = jnp.sqrt(dist_sq)
    kern_vals = signal_scalar * (1.0 + root_five * distance + 5.0 / 3.0 * dist_sq) * jnp.exp(-root_five * distance)
    return kern_vals.astype(jnp.bfloat16)

def apply_rows(row_pts, col_pts, col_sq, vectors, signal_scalar):
    feature_count = row_pts.shape[0]
    row_count = row_pts.shape[1]
    block_len = math.gcd(row_count, 512)
    num_blocks = row_count // block_len
    blocks = row_pts.reshape(feature_count, num_blocks, block_len).transpose(1, 0, 2)

    def one_block(row_blk):
        kern_vals = matern_block(row_blk, square_norms(row_blk), col_pts, col_sq, signal_scalar)
        return lax.dot_general(vectors, kern_vals, contract_last, preferred_element_type=jnp.float32)
    result = lax.map(one_block, blocks)
    return result.transpose(1, 0, 2).reshape(vectors.shape[0], row_count)

def reference(points, candidates, length_scales, signal_var, noise_var, cand_prior, weights, residual, direction):
    scaled = (points / length_scales[:, None]).astype(jnp.bfloat16)
    cand_scaled = (candidates / length_scales[:, None]).astype(jnp.bfloat16)
    signal_scalar = signal_var[0]
    col_sq = square_norms(scaled)
    dir_low = direction.astype(jnp.bfloat16)
    kernel_out = apply_rows(scaled, scaled, col_sq, dir_low, signal_scalar)
    image_vec = kernel_out + noise_var[0] * direction
    norm_now = lax.optimization_barrier(jnp.sum(residual * residual, axis=1))
    curvature = lax.optimization_barrier(jnp.sum(direction * image_vec, axis=1))
    step_len = norm_now / curvature
    weights_new = weights + step_len[:, None] * direction
    residual_new = residual - step_len[:, None] * image_vec
    norm_next = lax.optimization_barrier(jnp.sum(residual_new * residual_new, axis=1))
    direction_new = residual_new + (norm_next / norm_now)[:, None] * direction
    w_low = weights_new.astype(jnp.bfloat16)
    fitted = apply_rows(cand_scaled, scaled, col_sq, w_low, signal_scalar)
    cand_fit = cand_prior[None, :] + fitted
    return (weights_new, residual_new, direction_new, cand_fit)
```

```python
import functools
import math

import jax
import jax.numpy as jnp
from jax import lax
from jax.experimental import pallas as pl
from jax.experimental.pallas import tpu as pltpu
from jax.sharding import PartitionSpec as P

MESH = pl.DeviceIdType.MESH
f32 = jnp.float32
bf16 = jnp.bfloat16
LOG2E = math.log2(math.e)


def flip(index, step, size):
    total, bit = 0, 1
    while bit < size:
        total = total + bit * lax.rem(lax.div(index, bit) + lax.div(step, bit), 2)
        bit *= 2
    return total


def split3(x):
    hi = x.astype(bf16).astype(f32)
    mid = (x - hi).astype(bf16).astype(f32)
    return hi, mid, x - hi - mid


def norm_tail(sq, ones_first, one):
    n = sq.shape[1]
    row = lax.broadcasted_iota(jnp.int32, (16, n), 0)
    base = 3 if ones_first else 0
    const = 0 if ones_first else 3
    out = jnp.where((row >= const) & (row < const + 3), f32(one), f32(0))
    for k, piece in enumerate(split3(sq)):
        out = jnp.where(row == base + k, jnp.broadcast_to(piece, (16, n)), out)
    return out.astype(bf16)


def row_operand(a):
    sq = 5.0 * jnp.sum(a * a, axis=0, keepdims=True)
    return jnp.concatenate(
        [(-8.0 * a).astype(bf16), (-2.0 * a).astype(bf16), norm_tail(sq, False, 5.0)], axis=0
    )


def col_operand(b):
    wide = b.astype(f32)
    sq = jnp.sum(wide * wide, axis=0, keepdims=True)
    return jnp.concatenate([b, b, norm_tail(sq, True, 1.0)], axis=0)


def matern(v):
    v = jnp.maximum(v, 1e-30)
    u = v * lax.rsqrt(v)
    return ((1.0 + u + v * f32(1.0 / 3.0)) * jnp.exp2(u * f32(-LOG2E))).astype(bf16)


def kernel(
    R, C,
    pts_hbm, cand_hbm, ls_hbm, sig_ref, noise_ref, prior_hbm, w_hbm, r_hbm, d_hbm,
    wn_ref, rn_ref, dn_ref, cf_ref,
    pts_v, cand_v, ls_v, prior_v, w_v, r_v, d_v,
    b_all, a_pts, a_cand, a_op, part, part_in, cpart, cout, cin, st_a, st_b,
    in_sem, b_send, b_recv, a_send, a_recv, c_send, c_recv,
    p_send, p_recv, q_send, q_recv, s_send, s_recv, t_send, t_recv,
):
    row = lax.axis_index("row")
    col = lax.axis_index("col")
    L = pts_v.shape[1]
    Q = cand_v.shape[1]

    loads = [
        pltpu.make_async_copy(src, dst, in_sem.at[i])
        for i, (src, dst) in enumerate(
            [(ls_hbm, ls_v), (pts_hbm, pts_v), (cand_hbm, cand_v), (d_hbm, d_v),
             (w_hbm, w_v), (r_hbm, r_v), (prior_hbm, prior_v)]
        )
    ]
    for copy in loads:
        copy.start()

    barrier = pltpu.get_barrier_semaphore()
    for k in range(1, C):
        pl.semaphore_signal(barrier, inc=1, device_id=(row, flip(col, k, C)), device_id_type=MESH)
    for k in range(1, R):
        pl.semaphore_signal(barrier, inc=1, device_id=(flip(row, k, R), col), device_id_type=MESH)

    def col_copy(k, src, dst, send, recv):
        peer = flip(col, k, C)
        return pltpu.make_async_remote_copy(
            src_ref=src, dst_ref=dst.at[col], send_sem=send.at[k], recv_sem=recv.at[col],
            device_id=(row, peer), device_id_type=MESH,
        )

    def col_arrive(k, dst, recv):
        peer = flip(col, k, C)
        pltpu.make_async_remote_copy(
            src_ref=dst.at[peer], dst_ref=dst.at[peer], send_sem=recv.at[peer],
            recv_sem=recv.at[peer], device_id=(row, peer), device_id_type=MESH,
        ).wait_recv()

    def row_copy(k, src, dst, send, recv):
        peer = flip(row, k, R)
        return pltpu.make_async_remote_copy(
            src_ref=src, dst_ref=dst.at[row], send_sem=send.at[k], recv_sem=recv.at[row],
            device_id=(peer, col), device_id_type=MESH,
        )

    def row_arrive(k, dst, recv):
        peer = flip(row, k, R)
        pltpu.make_async_remote_copy(
            src_ref=dst.at[peer], dst_ref=dst.at[peer], send_sem=recv.at[peer],
            recv_sem=recv.at[peer], device_id=(peer, col), device_id_type=MESH,
        ).wait_recv()

    for copy in loads[:3]:
        copy.wait()
    eye = lax.broadcasted_iota(jnp.int32, (32, 32), 0) == lax.broadcasted_iota(jnp.int32, (32, 32), 1)
    scale = jnp.sum(jnp.where(eye, jnp.broadcast_to(ls_v[...], (32, 32)), 0.0), axis=1, keepdims=True)
    scaled = (pts_v[...] / scale).astype(bf16)
    b_all[row, 0:32, :] = scaled
    a_pts[col] = scaled
    a_cand[col] = (cand_v[...] / scale).astype(bf16)
    for copy in loads[3:]:
        copy.wait()
    b_all[row, 32:48, :] = d_v[...].astype(bf16)
    b_all[row, 48:64, :] = w_v[...].astype(bf16)

    pl.semaphore_wait(barrier, C - 1 + R - 1)
    sends = []
    for k in range(1, C):
        sends.append(col_copy(k, a_pts.at[col], a_pts, a_send, a_recv))
        sends[-1].start()
        sends.append(col_copy(k, a_cand.at[col], a_cand, c_send, c_recv))
        sends[-1].start()
    for k in range(1, R):
        sends.append(row_copy(k, b_all.at[row], b_all, b_send, b_recv))
        sends[-1].start()

    part[...] = jnp.zeros_like(part)
    cpart[...] = jnp.zeros_like(cpart)

    for k in range(1, C):
        col_arrive(k, a_pts, a_recv)
        col_arrive(k, a_cand, c_recv)
    for k in range(C):
        a_op[k] = row_operand(a_pts[k].astype(f32))
    per_tile = L // Q
    tiles = C // per_tile
    for t in range(tiles):
        wide = None
        for k in range(per_tile):
            place = (
                lax.broadcasted_iota(jnp.int32, (Q, L), 1)
                == lax.broadcasted_iota(jnp.int32, (Q, L), 0) + k * Q
            ).astype(f32).astype(bf16)
            term = jnp.dot(a_cand[t * per_tile + k], place, preferred_element_type=f32)
            wide = term if wide is None else wide + term
        a_op[C + t] = row_operand(wide)

    def chunk(src):
        b_op = col_operand(b_all[src, 0:32, :])
        d_low = b_all[src, 32:48, :]
        both = b_all[src, 32:64, :]
        for t in range(C + tiles):
            v = lax.dot_general(
                b_op, a_op[t], (((0,), (0,)), ((), ())), preferred_element_type=f32
            )
            kern = matern(v)
            if t < C:
                part[t] += jnp.dot(d_low, kern, preferred_element_type=f32)
            else:
                cpart[t - C] += jnp.dot(both, kern, preferred_element_type=f32)

    chunk(row)

    def step(k, carry):
        row_arrive(k, b_all, b_recv)
        chunk(flip(row, k, R))
        return carry

    lax.fori_loop(1, R, step, 0)

    for k in range(1, C):
        sends.append(col_copy(k, part.at[flip(col, k, C)], part_in, p_send, p_recv))
        sends[-1].start()
    for t in range(tiles):
        for k in range(per_tile):
            cout[t * per_tile + k] = cpart[t, :, k * Q:(k + 1) * Q]
    for k in range(1, C):
        sends.append(col_copy(k, cout.at[flip(col, k, C)], cin, q_send, q_recv))
        sends[-1].start()

    signal = sig_ref[0]
    d = d_v[...]
    r = r_v[...]
    total = part[col]
    for k in range(1, C):
        col_arrive(k, part_in, p_recv)
        total = total + part_in[flip(col, k, C)]
    image = signal * total + noise_ref[0] * d

    lane = lax.broadcasted_iota(jnp.int32, (16, 128), 1)
    sub = lax.broadcasted_iota(jnp.int32, (16, 128), 0)
    packed = jnp.zeros((16, 128), f32)
    for q, product in enumerate((r * r, d * image, r * image, image * image)):
        value = jnp.sum(product, axis=1, keepdims=True)
        packed = packed + jnp.where(lane == sub + 16 * q, value, 0.0)
    packed = jnp.sum(packed, axis=0, keepdims=True)

    st_a[col] = packed
    for k in range(1, C):
        sends.append(col_copy(k, st_a.at[col], st_a, s_send, s_recv))
        sends[-1].start()
    for k in range(1, C):
        col_arrive(k, st_a, s_recv)
    st_b[row] = jnp.sum(st_a[...], axis=0)
    for k in range(1, R):
        sends.append(row_copy(k, st_b.at[row], st_b, t_send, t_recv))
        sends[-1].start()

    fit = cout[col]
    for k in range(1, C):
        col_arrive(k, cin, q_recv)
        fit = fit + cin[flip(col, k, C)]

    for k in range(1, R):
        row_arrive(k, st_b, t_recv)
    sums = jnp.broadcast_to(jnp.sum(st_b[...], axis=0), (16, 128))

    def column(q):
        return jnp.sum(jnp.where(lane == sub + 16 * q, sums, 0.0), axis=1, keepdims=True)

    norm_now, curvature, cross, image_sq = column(0), column(1), column(2), column(3)
    step_len = norm_now / curvature
    norm_next = jnp.maximum(norm_now - 2.0 * (step_len * cross) + step_len * (step_len * image_sq), 0.0)
    r_new = r - step_len * image
    wn_ref[...] = w_v[...] + step_len * d
    rn_ref[...] = r_new
    dn_ref[...] = r_new + (norm_next / norm_now) * d
    cf_ref[...] = prior_v[...] + signal * (fit[16:32] + step_len * fit[0:16])
    for copy in sends:
        copy.wait_send()


def per_device(R, C, points, candidates, length_scales, signal_var, noise_var, cand_prior, weights, residual, direction):
    F, L = points.shape
    Q = candidates.shape[1]
    cols = weights.shape[0]
    tiles = C * Q // L
    hbm = pl.BlockSpec(memory_space=pl.ANY)
    smem = pl.BlockSpec(memory_space=pltpu.SMEM)
    vmem = pl.BlockSpec(memory_space=pltpu.VMEM)
    dma = pltpu.SemaphoreType.DMA
    state = jax.ShapeDtypeStruct((cols, L), f32)
    return pl.pallas_call(
        functools.partial(kernel, R, C),
        out_shape=(state, state, state, jax.ShapeDtypeStruct((cols, Q), f32)),
        in_specs=[hbm, hbm, hbm, smem, smem, hbm, hbm, hbm, hbm],
        out_specs=(vmem, vmem, vmem, vmem),
        scratch_shapes=[
            pltpu.VMEM((F, L), f32),
            pltpu.VMEM((F, Q), f32),
            pltpu.VMEM((1, F), f32),
            pltpu.VMEM((1, Q), f32),
            pltpu.VMEM((cols, L), f32),
            pltpu.VMEM((cols, L), f32),
            pltpu.VMEM((cols, L), f32),
            pltpu.VMEM((R, F + 2 * cols, L), bf16),
            pltpu.VMEM((C, F, L), bf16),
            pltpu.VMEM((C, F, Q), bf16),
            pltpu.VMEM((C + tiles, 2 * F + 16, L), bf16),
            pltpu.VMEM((C, cols, L), f32),
            pltpu.VMEM((C, cols, L), f32),
            pltpu.VMEM((tiles, 2 * cols, L), f32),
            pltpu.VMEM((C, 2 * cols, Q), f32),
            pltpu.VMEM((C, 2 * cols, Q), f32),
            pltpu.VMEM((C, 1, 128), f32),
            pltpu.VMEM((R, 1, 128), f32),
            dma((7,)),
            dma((R,)), dma((R,)),
            dma((C,)), dma((C,)),
            dma((C,)), dma((C,)),
            dma((C,)), dma((C,)),
            dma((C,)), dma((C,)),
            dma((C,)), dma((C,)),
            dma((R,)), dma((R,)),
        ],
        compiler_params=pltpu.CompilerParams(
            collective_id=0, has_side_effects=True, vmem_limit_bytes=48 * 1024 * 1024
        ),
    )(
        points, candidates, length_scales[None, :], signal_var, noise_var,
        cand_prior[None, :], weights, residual, direction,
    )


def solution(mesh):
    split = P(None, ("row", "col"))
    return jax.shard_map(
        functools.partial(per_device, mesh.shape["row"], mesh.shape["col"]),
        mesh=mesh,
        in_specs=(split, split, P(), P(), P(), P(("row", "col")), split, split, split),
        out_specs=(split, split, split, split),
        check_vma=False,
    )
```

```python
import functools
import math

import jax
import jax.numpy as jnp
from jax import lax
from jax.experimental import pallas as pl
from jax.experimental.pallas import tpu as pltpu
from jax.sharding import PartitionSpec as P

MESH = pl.DeviceIdType.MESH
f32 = jnp.float32
bf16 = jnp.bfloat16
VMEM_LIMIT = 63 * 1024 * 1024
LOG2E = math.log2(math.e)


def flip(index, step, size):
    total, bit = 0, 1
    while bit < size:
        total = total + bit * lax.rem(lax.div(index, bit) + lax.div(step, bit), 2)
        bit *= 2
    return total


def split3(x):
    hi = x.astype(bf16).astype(f32)
    mid = (x - hi).astype(bf16).astype(f32)
    return hi, mid, x - hi - mid


def norm_tail(sq, ones_first, one):
    n = sq.shape[1]
    row = lax.broadcasted_iota(jnp.int32, (16, n), 0)
    base = 3 if ones_first else 0
    const = 0 if ones_first else 3
    out = jnp.where((row >= const) & (row < const + 3), f32(one), f32(0))
    for k, piece in enumerate(split3(sq)):
        out = jnp.where(row == base + k, jnp.broadcast_to(piece, (16, n)), out)
    return out.astype(bf16)


def row_operand(a):
    sq = 5.0 * jnp.sum(a * a, axis=0, keepdims=True)
    return jnp.concatenate(
        [(-8.0 * a).astype(bf16), (-2.0 * a).astype(bf16), norm_tail(sq, False, 5.0),
         jnp.zeros((48, a.shape[1]), bf16)], axis=0
    )


def col_operand(b):
    wide = b.astype(f32)
    sq = jnp.sum(wide * wide, axis=0, keepdims=True)
    fill = jnp.zeros((48, b.shape[1]), bf16)
    return jnp.concatenate([b, b, norm_tail(sq, True, 1.0), fill], axis=0).T


def matern(v):
    v = jnp.maximum(v, 1e-30)
    u = v * lax.rsqrt(v)
    return ((1.0 + u + v * f32(1.0 / 3.0)) * jnp.exp2(u * f32(-LOG2E))).astype(bf16)


def kernel(
    R, C,
    pts_hbm, cand_hbm, ls_hbm, sig_ref, noise_ref, prior_hbm, w_hbm, r_hbm, d_hbm,
    wn_ref, rn_ref, dn_ref, cf_ref,
    pts_v, cand_v, ls_v, prior_v, w_v, r_v, d_v,
    b_all, a_pts, a_cand, a_op, part, part_in, cpart, cout, cin, st_a, st_b,
    in_sem, b_send, b_recv, a_send, a_recv, c_send, c_recv,
    p_send, p_recv, q_send, q_recv, s_send, s_recv, t_send, t_recv,
):
    row = lax.axis_index("row")
    col = lax.axis_index("col")
    L = pts_v.shape[1]
    Q = cand_v.shape[1]

    loads = [
        pltpu.make_async_copy(src, dst, in_sem.at[i])
        for i, (src, dst) in enumerate(
            [(ls_hbm, ls_v), (pts_hbm, pts_v), (cand_hbm, cand_v), (d_hbm, d_v),
             (w_hbm, w_v), (r_hbm, r_v), (prior_hbm, prior_v)]
        )
    ]
    for copy in loads:
        copy.start()

    barrier = pltpu.get_barrier_semaphore()
    for k in range(1, C):
        pl.semaphore_signal(barrier, inc=1, device_id=(row, flip(col, k, C)), device_id_type=MESH)
    for k in range(1, R):
        pl.semaphore_signal(barrier, inc=1, device_id=(flip(row, k, R), col), device_id_type=MESH)

    def col_copy(k, src, dst, send, recv):
        peer = flip(col, k, C)
        return pltpu.make_async_remote_copy(
            src_ref=src, dst_ref=dst.at[col], send_sem=send.at[k], recv_sem=recv.at[col],
            device_id=(row, peer), device_id_type=MESH,
        )

    def col_arrive(k, dst, recv):
        peer = flip(col, k, C)
        pltpu.make_async_remote_copy(
            src_ref=dst.at[peer], dst_ref=dst.at[peer], send_sem=recv.at[peer],
            recv_sem=recv.at[peer], device_id=(row, peer), device_id_type=MESH,
        ).wait_recv()

    def row_copy(k, src, dst, send, recv):
        peer = flip(row, k, R)
        return pltpu.make_async_remote_copy(
            src_ref=src, dst_ref=dst.at[row], send_sem=send.at[k], recv_sem=recv.at[row],
            device_id=(peer, col), device_id_type=MESH,
        )

    def row_arrive(k, dst, recv):
        peer = flip(row, k, R)
        pltpu.make_async_remote_copy(
            src_ref=dst.at[peer], dst_ref=dst.at[peer], send_sem=recv.at[peer],
            recv_sem=recv.at[peer], device_id=(peer, col), device_id_type=MESH,
        ).wait_recv()

    for copy in loads[:3]:
        copy.wait()
    eye = lax.broadcasted_iota(jnp.int32, (32, 32), 0) == lax.broadcasted_iota(jnp.int32, (32, 32), 1)
    scale = jnp.sum(jnp.where(eye, jnp.broadcast_to(ls_v[...], (32, 32)), 0.0), axis=1, keepdims=True)
    scaled = (pts_v[...] / scale).astype(bf16)
    b_all[row, 0:32, :] = scaled
    a_pts[col] = scaled
    a_cand[col] = (cand_v[...] / scale).astype(bf16)
    for copy in loads[3:]:
        copy.wait()
    b_all[row, 32:48, :] = d_v[...].astype(bf16)
    b_all[row, 48:64, :] = w_v[...].astype(bf16)

    pl.semaphore_wait(barrier, C - 1 + R - 1)
    sends = []
    for k in range(1, C):
        sends.append(col_copy(k, a_pts.at[col], a_pts, a_send, a_recv))
        sends[-1].start()
        sends.append(col_copy(k, a_cand.at[col], a_cand, c_send, c_recv))
        sends[-1].start()
    for k in range(1, R):
        sends.append(row_copy(k, b_all.at[row], b_all, b_send, b_recv))
        sends[-1].start()

    part[...] = jnp.zeros_like(part)
    cpart[...] = jnp.zeros_like(cpart)

    for k in range(1, C):
        col_arrive(k, a_pts, a_recv)
        col_arrive(k, a_cand, c_recv)
    for k in range(C):
        a_op[k] = row_operand(a_pts[k].astype(f32))
    per_tile = L // Q
    tiles = C // per_tile
    for t in range(tiles):
        wide = None
        for k in range(per_tile):
            place = (
                lax.broadcasted_iota(jnp.int32, (Q, L), 1)
                == lax.broadcasted_iota(jnp.int32, (Q, L), 0) + k * Q
            ).astype(f32).astype(bf16)
            term = jnp.dot(a_cand[t * per_tile + k], place, preferred_element_type=f32)
            wide = term if wide is None else wide + term
        a_op[C + t] = row_operand(wide)

    def chunk(src):
        b_op = col_operand(b_all[src, 0:32, :])
        d_low = b_all[src, 32:48, :]
        both = b_all[src, 32:64, :]
        for t in range(C + tiles):
            v = jnp.dot(b_op, a_op[t], preferred_element_type=f32)
            kern = matern(v)
            if t < C:
                part[t] += jnp.dot(d_low, kern, preferred_element_type=f32)
            else:
                cpart[t - C] += jnp.dot(both, kern, preferred_element_type=f32)

    chunk(row)

    def step(k, carry):
        row_arrive(k, b_all, b_recv)
        chunk(flip(row, k, R))
        return carry

    lax.fori_loop(1, R, step, 0)

    for k in range(1, C):
        sends.append(col_copy(k, part.at[flip(col, k, C)], part_in, p_send, p_recv))
        sends[-1].start()
    for t in range(tiles):
        for k in range(per_tile):
            cout[t * per_tile + k] = cpart[t, :, k * Q:(k + 1) * Q]
    for k in range(1, C):
        sends.append(col_copy(k, cout.at[flip(col, k, C)], cin, q_send, q_recv))
        sends[-1].start()

    signal = sig_ref[0]
    d = d_v[...]
    r = r_v[...]
    total = part[col]
    for k in range(1, C):
        col_arrive(k, part_in, p_recv)
        total = total + part_in[flip(col, k, C)]
    image = signal * total + noise_ref[0] * d

    lane = lax.broadcasted_iota(jnp.int32, (16, 128), 1)
    sub = lax.broadcasted_iota(jnp.int32, (16, 128), 0)
    packed = jnp.zeros((16, 128), f32)
    for q, product in enumerate((r * r, d * image, r * image, image * image)):
        value = jnp.sum(product, axis=1, keepdims=True)
        packed = packed + jnp.where(lane == sub + 16 * q, value, 0.0)
    packed = jnp.sum(packed, axis=0, keepdims=True)

    st_a[col] = packed
    for k in range(1, C):
        sends.append(col_copy(k, st_a.at[col], st_a, s_send, s_recv))
        sends[-1].start()
    for k in range(1, C):
        col_arrive(k, st_a, s_recv)
    st_b[row] = jnp.sum(st_a[...], axis=0)
    for k in range(1, R):
        sends.append(row_copy(k, st_b.at[row], st_b, t_send, t_recv))
        sends[-1].start()

    fit = cout[col]
    for k in range(1, C):
        col_arrive(k, cin, q_recv)
        fit = fit + cin[flip(col, k, C)]

    for k in range(1, R):
        row_arrive(k, st_b, t_recv)
    sums = jnp.broadcast_to(jnp.sum(st_b[...], axis=0), (16, 128))

    def column(q):
        return jnp.sum(jnp.where(lane == sub + 16 * q, sums, 0.0), axis=1, keepdims=True)

    norm_now, curvature, cross, image_sq = column(0), column(1), column(2), column(3)
    step_len = norm_now / curvature
    norm_next = jnp.maximum(norm_now - 2.0 * (step_len * cross) + step_len * (step_len * image_sq), 0.0)
    r_new = r - step_len * image
    wn_ref[...] = w_v[...] + step_len * d
    rn_ref[...] = r_new
    dn_ref[...] = r_new + (norm_next / norm_now) * d
    cf_ref[...] = prior_v[...] + signal * (fit[16:32] + step_len * fit[0:16])
    for copy in sends:
        copy.wait_send()


def hand_over(*refs):
    sem = refs[8]
    copies = [pltpu.make_async_copy(refs[i], refs[4 + i], sem.at[i]) for i in range(4)]
    for copy in copies:
        copy.start()
    for copy in copies:
        copy.wait()


def per_device(R, C, points, candidates, length_scales, signal_var, noise_var, cand_prior, weights, residual, direction):
    F, L = points.shape
    Q = candidates.shape[1]
    cols = weights.shape[0]
    tiles = C * Q // L
    hbm = pl.BlockSpec(memory_space=pl.ANY)
    smem = pl.BlockSpec(memory_space=pltpu.SMEM)
    vmem = pl.BlockSpec(memory_space=pltpu.VMEM)
    dma = pltpu.SemaphoreType.DMA
    state = jax.ShapeDtypeStruct((cols, L), f32)
    shapes = (state, state, state, jax.ShapeDtypeStruct((cols, Q), f32))
    results = pl.pallas_call(
        functools.partial(kernel, R, C),
        out_shape=shapes,
        in_specs=[hbm, hbm, hbm, smem, smem, hbm, hbm, hbm, hbm],
        out_specs=(vmem, vmem, vmem, vmem),
        scratch_shapes=[
            pltpu.VMEM((F, L), f32),
            pltpu.VMEM((F, Q), f32),
            pltpu.VMEM((1, F), f32),
            pltpu.VMEM((1, Q), f32),
            pltpu.VMEM((cols, L), f32),
            pltpu.VMEM((cols, L), f32),
            pltpu.VMEM((cols, L), f32),
            pltpu.VMEM((R, F + 2 * cols, L), bf16),
            pltpu.VMEM((C, F, L), bf16),
            pltpu.VMEM((C, F, Q), bf16),
            pltpu.VMEM((C + tiles, 128, L), bf16),
            pltpu.VMEM((C, cols, L), f32),
            pltpu.VMEM((C, cols, L), f32),
            pltpu.VMEM((tiles, 2 * cols, L), f32),
            pltpu.VMEM((C, 2 * cols, Q), f32),
            pltpu.VMEM((C, 2 * cols, Q), f32),
            pltpu.VMEM((C, 1, 128), f32),
            pltpu.VMEM((R, 1, 128), f32),
            dma((7,)),
            dma((R,)), dma((R,)),
            dma((C,)), dma((C,)),
            dma((C,)), dma((C,)),
            dma((C,)), dma((C,)),
            dma((C,)), dma((C,)),
            dma((C,)), dma((C,)),
            dma((R,)), dma((R,)),
        ],
        compiler_params=pltpu.CompilerParams(
            collective_id=0, has_side_effects=True, vmem_limit_bytes=VMEM_LIMIT
        ),
    )(
        points, candidates, length_scales[None, :], signal_var, noise_var,
        cand_prior[None, :], weights, residual, direction,
    )
    return pl.pallas_call(
        hand_over,
        out_shape=shapes,
        in_specs=[hbm] * 4,
        out_specs=(hbm,) * 4,
        scratch_shapes=[dma((4,))],
        compiler_params=pltpu.CompilerParams(vmem_limit_bytes=VMEM_LIMIT),
    )(*results)


def solution(mesh):
    split = P(None, ("row", "col"))
    return jax.shard_map(
        functools.partial(per_device, mesh.shape["row"], mesh.shape["col"]),
        mesh=mesh,
        in_specs=(split, split, P(), P(), P(), P(("row", "col")), split, split, split),
        out_specs=(split, split, split, split),
        check_vma=False,
    )
```

```python
import functools
import math

import jax
import jax.numpy as jnp
from jax import lax
from jax.experimental import pallas as pl
from jax.experimental.pallas import tpu as pltpu
from jax.sharding import PartitionSpec as P

MESH = pl.DeviceIdType.MESH
f32 = jnp.float32
bf16 = jnp.bfloat16
VMEM_LIMIT = 63 * 1024 * 1024
LOG2E = math.log2(math.e)


def flip(index, step, size):
    total, bit = 0, 1
    while bit < size:
        total = total + bit * lax.rem(lax.div(index, bit) + lax.div(step, bit), 2)
        bit *= 2
    return total


def split3(x):
    hi = x.astype(bf16).astype(f32)
    mid = (x - hi).astype(bf16).astype(f32)
    return hi, mid, x - hi - mid


def norm_tail(sq, ones_first, one):
    n = sq.shape[1]
    row = lax.broadcasted_iota(jnp.int32, (16, n), 0)
    base = 3 if ones_first else 0
    const = 0 if ones_first else 3
    out = jnp.where((row >= const) & (row < const + 3), f32(one), f32(0))
    for k, piece in enumerate(split3(sq)):
        out = jnp.where(row == base + k, jnp.broadcast_to(piece, (16, n)), out)
    return out.astype(bf16)


def row_operand(a):
    sq = 5.0 * jnp.sum(a * a, axis=0, keepdims=True)
    return jnp.concatenate(
        [(-8.0 * a).astype(bf16), (-2.0 * a).astype(bf16), norm_tail(sq, False, 5.0),
         jnp.zeros((48, a.shape[1]), bf16)], axis=0
    )


def col_operand(b):
    wide = b.astype(f32)
    sq = jnp.sum(wide * wide, axis=0, keepdims=True)
    fill = jnp.zeros((48, b.shape[1]), bf16)
    return jnp.concatenate([b, b, norm_tail(sq, True, 1.0), fill], axis=0).T


def matern(v):
    v = jnp.maximum(v, 1e-30)
    u = v * lax.rsqrt(v)
    return ((1.0 + u + v * f32(1.0 / 3.0)) * jnp.exp2(u * f32(-LOG2E))).astype(bf16)


def kernel(
    R, C,
    pts_hbm, cand_hbm, ls_hbm, sig_ref, noise_ref, prior_hbm, w_hbm, r_hbm, d_hbm,
    wn_ref, rn_ref, dn_ref, cf_ref,
    pts_v, cand_v, ls_v, prior_v, w_v, r_v, d_v,
    b_all, a_pts, a_cand, a_op, part, part_in, cpart, cout, cin, st,
    in_sem, b_send, b_recv, a_send, a_recv, c_send, c_recv,
    p_send, p_recv, q_send, q_recv, s_send, s_recv,
):
    row = lax.axis_index("row")
    col = lax.axis_index("col")
    L = pts_v.shape[1]
    Q = cand_v.shape[1]

    loads = [
        pltpu.make_async_copy(src, dst, in_sem.at[i])
        for i, (src, dst) in enumerate(
            [(ls_hbm, ls_v), (pts_hbm, pts_v), (cand_hbm, cand_v), (d_hbm, d_v),
             (w_hbm, w_v), (r_hbm, r_v), (prior_hbm, prior_v)]
        )
    ]
    for copy in loads:
        copy.start()

    barrier = pltpu.get_barrier_semaphore()
    def greet(k, carry):
        pl.semaphore_signal(
            barrier, inc=1, device_id=(flip(row, k // C, R), flip(col, k % C, C)), device_id_type=MESH
        )
        return carry

    lax.fori_loop(1, R * C, greet, 0)

    def col_copy(k, src, dst, send, recv):
        peer = flip(col, k, C)
        return pltpu.make_async_remote_copy(
            src_ref=src, dst_ref=dst.at[col], send_sem=send.at[k], recv_sem=recv.at[col],
            device_id=(row, peer), device_id_type=MESH,
        )

    def col_arrive(k, dst, recv):
        peer = flip(col, k, C)
        pltpu.make_async_remote_copy(
            src_ref=dst.at[peer], dst_ref=dst.at[peer], send_sem=recv.at[peer],
            recv_sem=recv.at[peer], device_id=(row, peer), device_id_type=MESH,
        ).wait_recv()

    def row_copy(k, src, dst, send, recv):
        peer = flip(row, k, R)
        return pltpu.make_async_remote_copy(
            src_ref=src, dst_ref=dst.at[row], send_sem=send.at[k], recv_sem=recv.at[row],
            device_id=(peer, col), device_id_type=MESH,
        )

    def row_arrive(k, dst, recv):
        peer = flip(row, k, R)
        pltpu.make_async_remote_copy(
            src_ref=dst.at[peer], dst_ref=dst.at[peer], send_sem=recv.at[peer],
            recv_sem=recv.at[peer], device_id=(peer, col), device_id_type=MESH,
        ).wait_recv()

    for copy in loads[:3]:
        copy.wait()
    eye = lax.broadcasted_iota(jnp.int32, (32, 32), 0) == lax.broadcasted_iota(jnp.int32, (32, 32), 1)
    scale = jnp.sum(jnp.where(eye, jnp.broadcast_to(ls_v[...], (32, 32)), 0.0), axis=1, keepdims=True)
    scaled = (pts_v[...] / scale).astype(bf16)
    b_all[row, 0:32, :] = scaled
    a_pts[col] = scaled
    a_cand[col] = (cand_v[...] / scale).astype(bf16)
    for copy in loads[3:]:
        copy.wait()
    b_all[row, 32:48, :] = d_v[...].astype(bf16)
    b_all[row, 48:64, :] = w_v[...].astype(bf16)

    pl.semaphore_wait(barrier, R * C - 1)
    sends = []
    for k in range(1, C):
        sends.append(col_copy(k, a_pts.at[col], a_pts, a_send, a_recv))
        sends[-1].start()
        sends.append(col_copy(k, a_cand.at[col], a_cand, c_send, c_recv))
        sends[-1].start()
    direct = list(range(2, R, 2)) + [1]
    for k in direct:
        sends.append(row_copy(k, b_all.at[row], b_all, b_send, b_recv))
        sends[-1].start()

    part[...] = jnp.zeros_like(part)
    cpart[...] = jnp.zeros_like(cpart)

    per_tile = L // Q
    tiles = C // per_tile

    def prepare(src):
        return col_operand(b_all[src, 0:32, :]), b_all[src, 32:48, :], b_all[src, 32:64, :]

    def run_tile(t, chunk):
        kern = matern(jnp.dot(chunk[0], a_op[t], preferred_element_type=f32))
        part[t] += jnp.dot(chunk[1], kern, preferred_element_type=f32)

    def cand_tile(t, chunk):
        kern = matern(jnp.dot(chunk[0], a_op[C + t], preferred_element_type=f32))
        cpart[t] += jnp.dot(chunk[2], kern, preferred_element_type=f32)

    own = prepare(row)
    a_op[col] = row_operand(a_pts[col].astype(f32))
    run_tile(col, own)
    for k in range(1, C):
        peer = flip(col, k, C)
        col_arrive(k, a_pts, a_recv)
        a_op[peer] = row_operand(a_pts[peer].astype(f32))
        run_tile(peer, own)
    for k in range(1, C):
        col_arrive(k, a_cand, c_recv)
    for t in range(tiles):
        wide = None
        for k in range(per_tile):
            place = (
                lax.broadcasted_iota(jnp.int32, (Q, L), 1)
                == lax.broadcasted_iota(jnp.int32, (Q, L), 0) + k * Q
            ).astype(f32).astype(bf16)
            term = jnp.dot(a_cand[t * per_tile + k], place, preferred_element_type=f32)
            wide = term if wide is None else wide + term
        a_op[C + t] = row_operand(wide)
        cand_tile(t, own)

    def whole_chunk(k):
        chunk = prepare(flip(row, k, R))
        for t in range(C):
            run_tile(t, chunk)
        for t in range(tiles):
            cand_tile(t, chunk)

    def forward(k):
        src = flip(row, k, R)
        return pltpu.make_async_remote_copy(
            src_ref=b_all.at[src], dst_ref=b_all.at[src], send_sem=b_send.at[k + 1],
            recv_sem=b_recv.at[src], device_id=(flip(row, 1, R), col), device_id_type=MESH,
        )

    def step_direct(i, carry):
        k = 2 * i
        row_arrive(k, b_all, b_recv)
        forward(k).start()
        whole_chunk(k)
        return carry

    def step_forwarded(i, carry):
        k = 2 * i + 1
        row_arrive(k, b_all, b_recv)
        whole_chunk(k)
        return carry

    lax.fori_loop(1, R // 2, step_direct, 0)
    lax.fori_loop(0, R // 2 - 2, step_forwarded, 0)
    for k in range(2, R, 2):
        sends.append(forward(k))

    last = []
    for k in (R - 3, R - 1):
        row_arrive(k, b_all, b_recv)
        last.append(prepare(flip(row, k, R)))
    for k in range(C - 1, 0, -1):
        peer = flip(col, k, C)
        for chunk in last:
            run_tile(peer, chunk)
        sends.append(col_copy(k, part.at[peer], part_in, p_send, p_recv))
        sends[-1].start()
    for t in range(tiles):
        for chunk in last:
            cand_tile(t, chunk)
        for k in range(per_tile):
            cout[t * per_tile + k] = cpart[t, :, k * Q:(k + 1) * Q]
    for k in range(1, C):
        sends.append(col_copy(k, cout.at[flip(col, k, C)], cin, q_send, q_recv))
        sends[-1].start()
    for chunk in last:
        run_tile(col, chunk)

    signal = sig_ref[0]
    d = d_v[...]
    r = r_v[...]
    total = part[col]
    for k in range(1, C):
        col_arrive(k, part_in, p_recv)
        total = total + part_in[flip(col, k, C)]
    image = signal * total + noise_ref[0] * d

    lane = lax.broadcasted_iota(jnp.int32, (16, 128), 1)
    sub = lax.broadcasted_iota(jnp.int32, (16, 128), 0)
    packed = jnp.zeros((16, 128), f32)
    for q, product in enumerate((r * r, d * image, r * image, image * image)):
        value = jnp.sum(product, axis=1, keepdims=True)
        packed = packed + jnp.where(lane == sub + 16 * q, value, 0.0)
    packed = jnp.sum(packed, axis=0, keepdims=True)

    me = row * C + col
    st[me] = packed

    def sums_copy(k):
        return pltpu.make_async_remote_copy(
            src_ref=st.at[me], dst_ref=st.at[me], send_sem=s_send.at[k], recv_sem=s_recv.at[me],
            device_id=(flip(row, k // C, R), flip(col, k % C, C)), device_id_type=MESH,
        )

    def sums_start(k, carry):
        sums_copy(k).start()
        return carry

    def sums_arrive(k, carry):
        peer = flip(row, k // C, R) * C + flip(col, k % C, C)
        pltpu.make_async_remote_copy(
            src_ref=st.at[peer], dst_ref=st.at[peer], send_sem=s_recv.at[peer],
            recv_sem=s_recv.at[peer],
            device_id=(flip(row, k // C, R), flip(col, k % C, C)), device_id_type=MESH,
        ).wait_recv()
        return carry

    def sums_sent(k, carry):
        sums_copy(k).wait_send()
        return carry

    lax.fori_loop(1, R * C, sums_start, 0)

    fit = cout[col]
    for k in range(1, C):
        col_arrive(k, cin, q_recv)
        fit = fit + cin[flip(col, k, C)]

    lax.fori_loop(1, R * C, sums_arrive, 0)
    sums = jnp.broadcast_to(jnp.sum(st[...], axis=0), (16, 128))

    def column(q):
        return jnp.sum(jnp.where(lane == sub + 16 * q, sums, 0.0), axis=1, keepdims=True)

    norm_now, curvature, cross, image_sq = column(0), column(1), column(2), column(3)
    step_len = norm_now / curvature
    norm_next = jnp.maximum(norm_now - 2.0 * (step_len * cross) + step_len * (step_len * image_sq), 0.0)
    r_new = r - step_len * image
    wn_ref[...] = w_v[...] + step_len * d
    rn_ref[...] = r_new
    dn_ref[...] = r_new + (norm_next / norm_now) * d
    cf_ref[...] = prior_v[...] + signal * (fit[16:32] + step_len * fit[0:16])
    for copy in sends:
        copy.wait_send()
    lax.fori_loop(1, R * C, sums_sent, 0)


def hand_over(*refs):
    for i in range(4):
        refs[4 + i][...] = refs[i][...]


def per_device(R, C, points, candidates, length_scales, signal_var, noise_var, cand_prior, weights, residual, direction):
    F, L = points.shape
    Q = candidates.shape[1]
    cols = weights.shape[0]
    tiles = C * Q // L
    hbm = pl.BlockSpec(memory_space=pl.ANY)
    smem = pl.BlockSpec(memory_space=pltpu.SMEM)
    vmem = pl.BlockSpec(memory_space=pltpu.VMEM)
    dma = pltpu.SemaphoreType.DMA
    state = jax.ShapeDtypeStruct((cols, L), f32)
    shapes = (state, state, state, jax.ShapeDtypeStruct((cols, Q), f32))
    results = pl.pallas_call(
        functools.partial(kernel, R, C),
        out_shape=shapes,
        in_specs=[hbm, hbm, hbm, smem, smem, hbm, hbm, hbm, hbm],
        out_specs=(vmem, vmem, vmem, vmem),
        scratch_shapes=[
            pltpu.VMEM((F, L), f32),
            pltpu.VMEM((F, Q), f32),
            pltpu.VMEM((1, F), f32),
            pltpu.VMEM((1, Q), f32),
            pltpu.VMEM((cols, L), f32),
            pltpu.VMEM((cols, L), f32),
            pltpu.VMEM((cols, L), f32),
            pltpu.VMEM((R, F + 2 * cols, L), bf16),
            pltpu.VMEM((C, F, L), bf16),
            pltpu.VMEM((C, F, Q), bf16),
            pltpu.VMEM((C + tiles, 128, L), bf16),
            pltpu.VMEM((C, cols, L), f32),
            pltpu.VMEM((C, cols, L), f32),
            pltpu.VMEM((tiles, 2 * cols, L), f32),
            pltpu.VMEM((C, 2 * cols, Q), f32),
            pltpu.VMEM((C, 2 * cols, Q), f32),
            pltpu.VMEM((R * C, 1, 128), f32),
            dma((7,)),
            dma((R,)), dma((R,)),
            dma((C,)), dma((C,)),
            dma((C,)), dma((C,)),
            dma((C,)), dma((C,)),
            dma((C,)), dma((C,)),
            dma((R * C,)), dma((R * C,)),
        ],
        compiler_params=pltpu.CompilerParams(
            collective_id=0, has_side_effects=True, vmem_limit_bytes=VMEM_LIMIT
        ),
    )(
        points, candidates, length_scales[None, :], signal_var, noise_var,
        cand_prior[None, :], weights, residual, direction,
    )
    return pl.pallas_call(
        hand_over,
        out_shape=shapes,
        in_specs=[vmem] * 4,
        out_specs=(vmem,) * 4,
        compiler_params=pltpu.CompilerParams(vmem_limit_bytes=VMEM_LIMIT),
    )(*results)


def solution(mesh):
    split = P(None, ("row", "col"))
    return jax.shard_map(
        functools.partial(per_device, mesh.shape["row"], mesh.shape["col"]),
        mesh=mesh,
        in_specs=(split, split, P(), P(), P(), P(("row", "col")), split, split, split),
        out_specs=(split, split, split, split),
        check_vma=False,
    )
```

```python
import functools
import math

import jax
import jax.numpy as jnp
from jax import lax
from jax.experimental import pallas as pl
from jax.experimental.pallas import tpu as pltpu
from jax.sharding import PartitionSpec as P

MESH = pl.DeviceIdType.MESH
f32 = jnp.float32
bf16 = jnp.bfloat16
PIECE = 32
VMEM_LIMIT = 63 * 1024 * 1024
LOG2E = math.log2(math.e)


def flip(index, step, size):
    total, bit = 0, 1
    while bit < size:
        total = total + bit * lax.rem(lax.div(index, bit) + lax.div(step, bit), 2)
        bit *= 2
    return total


def split3(x):
    hi = x.astype(bf16).astype(f32)
    mid = (x - hi).astype(bf16).astype(f32)
    return hi, mid, x - hi - mid


def norm_tail(sq, ones_first, one):
    n = sq.shape[1]
    row = lax.broadcasted_iota(jnp.int32, (16, n), 0)
    base = 3 if ones_first else 0
    const = 0 if ones_first else 3
    out = jnp.where((row >= const) & (row < const + 3), f32(one), f32(0))
    for k, piece in enumerate(split3(sq)):
        out = jnp.where(row == base + k, jnp.broadcast_to(piece, (16, n)), out)
    return out.astype(bf16)


def row_operand(a):
    sq = 5.0 * jnp.sum(a * a, axis=0, keepdims=True)
    return jnp.concatenate(
        [(-8.0 * a).astype(bf16), (-2.0 * a).astype(bf16), norm_tail(sq, False, 5.0),
         jnp.zeros((48, a.shape[1]), bf16)], axis=0
    )


def col_operand(b):
    wide = b.astype(f32)
    sq = jnp.sum(wide * wide, axis=0, keepdims=True)
    fill = jnp.zeros((48, b.shape[1]), bf16)
    return jnp.concatenate([b, b, norm_tail(sq, True, 1.0), fill], axis=0).T


def matern(v):
    v = jnp.maximum(v, 1e-30)
    u = v * lax.rsqrt(v)
    return ((1.0 + u + v * f32(1.0 / 3.0)) * jnp.exp2(u * f32(-LOG2E))).astype(bf16)


def kernel(
    R, C,
    pts_hbm, cand_hbm, ls_hbm, sig_ref, noise_ref, prior_hbm, w_hbm, r_hbm, d_hbm,
    wn_ref, rn_ref, dn_ref, cf_ref,
    pts_v, cand_v, ls_v, prior_v, w_v, r_v, d_v,
    b_all, a_pts, a_cand, a_op, v_buf, k_buf, acc, part_in, cout, cin, st,
    in_sem, b_send, b_recv, a_send, a_recv, c_send, c_recv,
    p_send, p_recv, q_send, q_recv, s_send, s_recv,
):
    row = lax.axis_index("row")
    col = lax.axis_index("col")
    L = pts_v.shape[1]
    Q = cand_v.shape[1]

    loads = [
        pltpu.make_async_copy(src, dst, in_sem.at[i])
        for i, (src, dst) in enumerate(
            [(ls_hbm, ls_v), (pts_hbm, pts_v), (cand_hbm, cand_v), (d_hbm, d_v),
             (w_hbm, w_v), (r_hbm, r_v), (prior_hbm, prior_v)]
        )
    ]
    for copy in loads:
        copy.start()

    barrier = pltpu.get_barrier_semaphore()
    def greet(k, carry):
        pl.semaphore_signal(
            barrier, inc=1, device_id=(flip(row, k // C, R), flip(col, k % C, C)), device_id_type=MESH
        )
        return carry

    lax.fori_loop(1, R * C, greet, 0)

    def col_copy(k, src, dst, send, recv):
        peer = flip(col, k, C)
        return pltpu.make_async_remote_copy(
            src_ref=src, dst_ref=dst.at[col], send_sem=send.at[k], recv_sem=recv.at[col],
            device_id=(row, peer), device_id_type=MESH,
        )

    def col_arrive(k, dst, recv):
        peer = flip(col, k, C)
        pltpu.make_async_remote_copy(
            src_ref=dst.at[peer], dst_ref=dst.at[peer], send_sem=recv.at[peer],
            recv_sem=recv.at[peer], device_id=(row, peer), device_id_type=MESH,
        ).wait_recv()

    def row_copy(k, src, dst, send, recv):
        peer = flip(row, k, R)
        return pltpu.make_async_remote_copy(
            src_ref=src, dst_ref=dst.at[row], send_sem=send.at[k], recv_sem=recv.at[row],
            device_id=(peer, col), device_id_type=MESH,
        )

    def row_arrive(k, dst, recv):
        peer = flip(row, k, R)
        pltpu.make_async_remote_copy(
            src_ref=dst.at[peer], dst_ref=dst.at[peer], send_sem=recv.at[peer],
            recv_sem=recv.at[peer], device_id=(peer, col), device_id_type=MESH,
        ).wait_recv()

    for copy in loads[:3]:
        copy.wait()
    eye = lax.broadcasted_iota(jnp.int32, (32, 32), 0) == lax.broadcasted_iota(jnp.int32, (32, 32), 1)
    scale = jnp.sum(jnp.where(eye, jnp.broadcast_to(ls_v[...], (32, 32)), 0.0), axis=1, keepdims=True)
    scaled = (pts_v[...] / scale).astype(bf16)
    b_all[row, 0:32, :] = scaled
    a_pts[col] = scaled
    a_cand[col] = (cand_v[...] / scale).astype(bf16)
    for copy in loads[3:]:
        copy.wait()
    b_all[row, 32:48, :] = d_v[...].astype(bf16)
    b_all[row, 48:64, :] = w_v[...].astype(bf16)

    pl.semaphore_wait(barrier, R * C - 1)
    sends = []
    for k in range(1, C):
        sends.append(col_copy(k, a_pts.at[col], a_pts, a_send, a_recv))
        sends[-1].start()
        sends.append(col_copy(k, a_cand.at[col], a_cand, c_send, c_recv))
        sends[-1].start()
    direct = list(range(2, R, 2)) + [1]
    for k in direct:
        sends.append(row_copy(k, b_all.at[row], b_all, b_send, b_recv))
        sends[-1].start()

    acc[...] = jnp.zeros_like(acc)

    per_tile = L // Q
    tiles = C // per_tile

    def prepare(src):
        return col_operand(b_all[src, 0:32, :]), b_all[src, 32:64, :]

    def run(chunks, first, end):
        jobs = [(t, i) for t in range(first, end) for i in range(len(chunks))]

        def inner(n):
            t, i = jobs[n]
            v_buf[n % 4] = jnp.dot(
                chunks[i][0], a_op[:, t * L:(t + 1) * L], preferred_element_type=f32
            )

        inner(0)
        for n, (t, i) in enumerate(jobs):
            if n + 1 < len(jobs):
                inner(n + 1)
            for p in range(0, L, PIECE):
                k_buf[n % 4, p:p + PIECE, :] = matern(v_buf[n % 4, p:p + PIECE, :])
            acc[:, t * L:(t + 1) * L] += jnp.dot(
                chunks[i][1], k_buf[n % 4], preferred_element_type=f32
            )

    def slot(k):
        start = (tiles + k) * L if k else 0
        return slice(start, start + L)

    own = prepare(row)
    a_op[:, slot(0)] = row_operand(a_pts[col].astype(f32))
    run([own], 0, 1)
    for k in range(1, C):
        col_arrive(k, a_pts, a_recv)
        a_op[:, slot(k)] = row_operand(a_pts[flip(col, k, C)].astype(f32))
    for k in range(1, C):
        col_arrive(k, a_cand, c_recv)
    for t in range(tiles):
        wide = None
        for k in range(per_tile):
            place = (
                lax.broadcasted_iota(jnp.int32, (Q, L), 1)
                == lax.broadcasted_iota(jnp.int32, (Q, L), 0) + k * Q
            ).astype(f32).astype(bf16)
            term = jnp.dot(
                a_cand[flip(col, t * per_tile + k, C)], place, preferred_element_type=f32
            )
            wide = term if wide is None else wide + term
        a_op[:, (1 + t) * L:(2 + t) * L] = row_operand(wide)
    run([own], 1, C + tiles)

    def whole_chunk(k):
        run([prepare(flip(row, k, R))], 0, C + tiles)

    def forward(k):
        src = flip(row, k, R)
        return pltpu.make_async_remote_copy(
            src_ref=b_all.at[src], dst_ref=b_all.at[src], send_sem=b_send.at[k + 1],
            recv_sem=b_recv.at[src], device_id=(flip(row, 1, R), col), device_id_type=MESH,
        )

    def step_direct(i, carry):
        k = 2 * i
        row_arrive(k, b_all, b_recv)
        forward(k).start()
        whole_chunk(k)
        return carry

    def step_forwarded(i, carry):
        k = 2 * i + 1
        row_arrive(k, b_all, b_recv)
        whole_chunk(k)
        return carry

    lax.fori_loop(1, R // 2, step_direct, 0)
    lax.fori_loop(0, R // 2 - 2, step_forwarded, 0)
    for k in range(2, R, 2):
        sends.append(forward(k))

    last = []
    for k in (R - 3, R - 1):
        row_arrive(k, b_all, b_recv)
        last.append(prepare(flip(row, k, R)))
    run(last, 1 + tiles, C + tiles)
    for k in range(C - 1, 0, -1):
        sends.append(col_copy(k, acc.at[0:16, slot(k)], part_in, p_send, p_recv))
        sends[-1].start()
    run(last, 0, 1 + tiles)
    for k in range(C):
        cout[k] = acc[:, L + k * Q:L + (k + 1) * Q]
    for k in range(1, C):
        sends.append(col_copy(k, cout.at[k], cin, q_send, q_recv))
        sends[-1].start()

    signal = sig_ref[0]
    d = d_v[...]
    r = r_v[...]
    total = acc[0:16, slot(0)]
    for k in range(1, C):
        col_arrive(k, part_in, p_recv)
        total = total + part_in[flip(col, k, C)]
    image = signal * total + noise_ref[0] * d

    lane = lax.broadcasted_iota(jnp.int32, (16, 128), 1)
    sub = lax.broadcasted_iota(jnp.int32, (16, 128), 0)
    packed = jnp.zeros((16, 128), f32)
    for q, product in enumerate((r * r, d * image, r * image, image * image)):
        value = jnp.sum(product, axis=1, keepdims=True)
        packed = packed + jnp.where(lane == sub + 16 * q, value, 0.0)
    packed = jnp.sum(packed, axis=0, keepdims=True)

    me = row * C + col
    st[me] = packed

    def sums_copy(k):
        return pltpu.make_async_remote_copy(
            src_ref=st.at[me], dst_ref=st.at[me], send_sem=s_send.at[k], recv_sem=s_recv.at[me],
            device_id=(flip(row, k // C, R), flip(col, k % C, C)), device_id_type=MESH,
        )

    def sums_start(k, carry):
        sums_copy(k).start()
        return carry

    def sums_arrive(k, carry):
        peer = flip(row, k // C, R) * C + flip(col, k % C, C)
        pltpu.make_async_remote_copy(
            src_ref=st.at[peer], dst_ref=st.at[peer], send_sem=s_recv.at[peer],
            recv_sem=s_recv.at[peer],
            device_id=(flip(row, k // C, R), flip(col, k % C, C)), device_id_type=MESH,
        ).wait_recv()
        return carry

    def sums_sent(k, carry):
        sums_copy(k).wait_send()
        return carry

    lax.fori_loop(1, R * C, sums_start, 0)

    fit = cout[0]
    for k in range(1, C):
        col_arrive(k, cin, q_recv)
        fit = fit + cin[flip(col, k, C)]

    lax.fori_loop(1, R * C, sums_arrive, 0)
    sums = jnp.broadcast_to(jnp.sum(st[...], axis=0), (16, 128))

    def column(q):
        return jnp.sum(jnp.where(lane == sub + 16 * q, sums, 0.0), axis=1, keepdims=True)

    norm_now, curvature, cross, image_sq = column(0), column(1), column(2), column(3)
    step_len = norm_now / curvature
    norm_next = jnp.maximum(norm_now - 2.0 * (step_len * cross) + step_len * (step_len * image_sq), 0.0)
    r_new = r - step_len * image
    wn_ref[...] = w_v[...] + step_len * d
    rn_ref[...] = r_new
    dn_ref[...] = r_new + (norm_next / norm_now) * d
    cf_ref[...] = prior_v[...] + signal * (fit[16:32] + step_len * fit[0:16])
    for copy in sends:
        copy.wait_send()
    lax.fori_loop(1, R * C, sums_sent, 0)


def hand_over(*refs):
    for i in range(4):
        refs[4 + i][...] = refs[i][...]


def per_device(R, C, points, candidates, length_scales, signal_var, noise_var, cand_prior, weights, residual, direction):
    F, L = points.shape
    Q = candidates.shape[1]
    cols = weights.shape[0]
    tiles = C * Q // L
    hbm = pl.BlockSpec(memory_space=pl.ANY)
    smem = pl.BlockSpec(memory_space=pltpu.SMEM)
    vmem = pl.BlockSpec(memory_space=pltpu.VMEM)
    dma = pltpu.SemaphoreType.DMA
    state = jax.ShapeDtypeStruct((cols, L), f32)
    shapes = (state, state, state, jax.ShapeDtypeStruct((cols, Q), f32))
    results = pl.pallas_call(
        functools.partial(kernel, R, C),
        out_shape=shapes,
        in_specs=[hbm, hbm, hbm, smem, smem, hbm, hbm, hbm, hbm],
        out_specs=(vmem, vmem, vmem, vmem),
        scratch_shapes=[
            pltpu.VMEM((F, L), f32),
            pltpu.VMEM((F, Q), f32),
            pltpu.VMEM((1, F), f32),
            pltpu.VMEM((1, Q), f32),
            pltpu.VMEM((cols, L), f32),
            pltpu.VMEM((cols, L), f32),
            pltpu.VMEM((cols, L), f32),
            pltpu.VMEM((R, F + 2 * cols, L), bf16),
            pltpu.VMEM((C, F, L), bf16),
            pltpu.VMEM((C, F, Q), bf16),
            pltpu.VMEM((128, (C + tiles) * L), bf16),
            pltpu.VMEM((4, L, L), f32),
            pltpu.VMEM((4, L, L), bf16),
            pltpu.VMEM((2 * cols, (C + tiles) * L), f32),
            pltpu.VMEM((C, cols, L), f32),
            pltpu.VMEM((C, 2 * cols, Q), f32),
            pltpu.VMEM((C, 2 * cols, Q), f32),
            pltpu.VMEM((R * C, 1, 128), f32),
            dma((7,)),
            dma((R,)), dma((R,)),
            dma((C,)), dma((C,)),
            dma((C,)), dma((C,)),
            dma((C,)), dma((C,)),
            dma((C,)), dma((C,)),
            dma((R * C,)), dma((R * C,)),
        ],
        compiler_params=pltpu.CompilerParams(
            collective_id=0, has_side_effects=True, vmem_limit_bytes=VMEM_LIMIT
        ),
    )(
        points, candidates, length_scales[None, :], signal_var, noise_var,
        cand_prior[None, :], weights, residual, direction,
    )
    return pl.pallas_call(
        hand_over,
        out_shape=shapes,
        in_specs=[vmem] * 4,
        out_specs=(vmem,) * 4,
        compiler_params=pltpu.CompilerParams(vmem_limit_bytes=VMEM_LIMIT),
    )(*results)


def solution(mesh):
    split = P(None, ("row", "col"))
    return jax.shard_map(
        functools.partial(per_device, mesh.shape["row"], mesh.shape["col"]),
        mesh=mesh,
        in_specs=(split, split, P(), P(), P(), P(("row", "col")), split, split, split),
        out_specs=(split, split, split, split),
        check_vma=False,
    )
```

```python
import functools
import math

import jax
import jax.numpy as jnp
from jax import lax
from jax.experimental import pallas as pl
from jax.experimental.pallas import tpu as pltpu
from jax.sharding import PartitionSpec as P

MESH = pl.DeviceIdType.MESH
f32 = jnp.float32
bf16 = jnp.bfloat16
PIECE = 32
VMEM_LIMIT = 63 * 1024 * 1024
LOG2E = math.log2(math.e)


def flip(index, step, size):
    total, bit = 0, 1
    while bit < size:
        total = total + bit * lax.rem(lax.div(index, bit) + lax.div(step, bit), 2)
        bit *= 2
    return total


def split3(x):
    hi = x.astype(bf16).astype(f32)
    mid = (x - hi).astype(bf16).astype(f32)
    return hi, mid, x - hi - mid


def norm_tail(sq, ones_first, one):
    n = sq.shape[1]
    row = lax.broadcasted_iota(jnp.int32, (16, n), 0)
    base = 3 if ones_first else 0
    const = 0 if ones_first else 3
    out = jnp.where((row >= const) & (row < const + 3), f32(one), f32(0))
    for k, piece in enumerate(split3(sq)):
        out = jnp.where(row == base + k, jnp.broadcast_to(piece, (16, n)), out)
    return out.astype(bf16)


def row_operand(a):
    sq = 5.0 * jnp.sum(a * a, axis=0, keepdims=True)
    return jnp.concatenate(
        [(-8.0 * a).astype(bf16), (-2.0 * a).astype(bf16), norm_tail(sq, False, 5.0),
         jnp.zeros((48, a.shape[1]), bf16)], axis=0
    )


def col_operand(b):
    wide = b.astype(f32)
    sq = jnp.sum(wide * wide, axis=0, keepdims=True)
    fill = jnp.zeros((48, b.shape[1]), bf16)
    return jnp.concatenate([b, b, norm_tail(sq, True, 1.0), fill], axis=0).T


def matern(v):
    v = jnp.maximum(v, 1e-30)
    u = v * lax.rsqrt(v)
    return ((1.0 + u + v * f32(1.0 / 3.0)) * jnp.exp2(u * f32(-LOG2E))).astype(bf16)


def kernel(
    R, C,
    pts_hbm, cand_hbm, ls_hbm, sig_ref, noise_ref, prior_hbm, w_hbm, r_hbm, d_hbm,
    wn_ref, rn_ref, dn_ref, cf_ref,
    pts_v, cand_v, ls_v, prior_v, w_v, r_v, d_v,
    b_all, a_pts, a_cand, a_op, v_buf, k_buf, acc, part_in, cout, cin, st,
    in_sem, b_send, b_recv, a_send, a_recv, c_send, c_recv,
    p_send, p_recv, q_send, q_recv, s_send, s_recv,
):
    row = lax.axis_index("row")
    col = lax.axis_index("col")
    L = pts_v.shape[1]
    Q = cand_v.shape[1]
    row_peer = [flip(row, k, R) for k in range(R)]
    col_peer = [flip(col, k, C) for k in range(C)]

    def row_of(k):
        return row_peer[k] if isinstance(k, int) else flip(row, k, R)

    loads = [
        pltpu.make_async_copy(src, dst, in_sem.at[i])
        for i, (src, dst) in enumerate(
            [(ls_hbm, ls_v), (pts_hbm, pts_v), (cand_hbm, cand_v), (d_hbm, d_v),
             (w_hbm, w_v), (r_hbm, r_v), (prior_hbm, prior_v)]
        )
    ]
    for copy in loads:
        copy.start()

    barrier = pltpu.get_barrier_semaphore()
    def everyone(visit):
        for b in range(1, C):
            visit(row, col_peer[b], b)

        def turn(a, carry):
            there = lax.rem(row + a, R)
            for b in range(C):
                visit(there, col_peer[b], a * C + b)
            return carry

        lax.fori_loop(1, R, turn, 0)

    everyone(lambda r, c, k: pl.semaphore_signal(
        barrier, inc=1, device_id=(r, c), device_id_type=MESH
    ))

    def col_copy(k, src, dst, send, recv):
        peer = col_peer[k]
        return pltpu.make_async_remote_copy(
            src_ref=src, dst_ref=dst.at[col], send_sem=send.at[k], recv_sem=recv.at[col],
            device_id=(row, peer), device_id_type=MESH,
        )

    def col_arrive(k, dst, recv):
        peer = col_peer[k]
        pltpu.make_async_remote_copy(
            src_ref=dst.at[peer], dst_ref=dst.at[peer], send_sem=recv.at[peer],
            recv_sem=recv.at[peer], device_id=(row, peer), device_id_type=MESH,
        ).wait_recv()

    def row_copy(k, src, dst, send, recv):
        peer = row_of(k)
        return pltpu.make_async_remote_copy(
            src_ref=src, dst_ref=dst.at[row], send_sem=send.at[k], recv_sem=recv.at[row],
            device_id=(peer, col), device_id_type=MESH,
        )

    def row_arrive(k, dst, recv):
        peer = row_of(k)
        pltpu.make_async_remote_copy(
            src_ref=dst.at[peer], dst_ref=dst.at[peer], send_sem=recv.at[peer],
            recv_sem=recv.at[peer], device_id=(peer, col), device_id_type=MESH,
        ).wait_recv()

    for copy in loads[:3]:
        copy.wait()
    eye = lax.broadcasted_iota(jnp.int32, (32, 32), 0) == lax.broadcasted_iota(jnp.int32, (32, 32), 1)
    scale = jnp.sum(jnp.where(eye, jnp.broadcast_to(ls_v[...], (32, 32)), 0.0), axis=1, keepdims=True)
    scaled = (pts_v[...] / scale).astype(bf16)
    b_all[row, 0:32, :] = scaled
    a_pts[col] = scaled
    a_cand[col] = (cand_v[...] / scale).astype(bf16)
    for copy in loads[3:]:
        copy.wait()
    b_all[row, 32:48, :] = d_v[...].astype(bf16)
    b_all[row, 48:64, :] = w_v[...].astype(bf16)

    pl.semaphore_wait(barrier, R * C - 1)
    sends = []
    for k in range(1, C):
        sends.append(col_copy(k, a_pts.at[col], a_pts, a_send, a_recv))
        sends[-1].start()
        sends.append(col_copy(k, a_cand.at[col], a_cand, c_send, c_recv))
        sends[-1].start()
    direct = list(range(2, R, 2)) + [1]
    for k in direct:
        sends.append(row_copy(k, b_all.at[row], b_all, b_send, b_recv))
        sends[-1].start()

    acc[...] = jnp.zeros_like(acc)

    per_tile = L // Q
    tiles = C // per_tile

    def prepare(src):
        return col_operand(b_all[src, 0:32, :]), b_all[src, 32:64, :]

    def run(chunks, first, end):
        jobs = [(t, i) for t in range(first, end) for i in range(len(chunks))]

        def inner(n):
            t, i = jobs[n]
            v_buf[n % 4] = jnp.dot(
                chunks[i][0], a_op[:, t * L:(t + 1) * L], preferred_element_type=f32
            )

        inner(0)
        for n, (t, i) in enumerate(jobs):
            if n + 1 < len(jobs):
                inner(n + 1)
            for p in range(0, L, PIECE):
                k_buf[n % 4, p:p + PIECE, :] = matern(v_buf[n % 4, p:p + PIECE, :])
            acc[:, t * L:(t + 1) * L] += jnp.dot(
                chunks[i][1], k_buf[n % 4], preferred_element_type=f32
            )

    def slot(k):
        start = (tiles + k) * L if k else 0
        return slice(start, start + L)

    own = prepare(row)
    a_op[:, slot(0)] = row_operand(a_pts[col].astype(f32))
    run([own], 0, 1)
    for k in range(1, C):
        col_arrive(k, a_pts, a_recv)
        a_op[:, slot(k)] = row_operand(a_pts[col_peer[k]].astype(f32))
    for k in range(1, C):
        col_arrive(k, a_cand, c_recv)
    for t in range(tiles):
        wide = None
        for k in range(per_tile):
            place = (
                lax.broadcasted_iota(jnp.int32, (Q, L), 1)
                == lax.broadcasted_iota(jnp.int32, (Q, L), 0) + k * Q
            ).astype(f32).astype(bf16)
            term = jnp.dot(
                a_cand[col_peer[t * per_tile + k]], place, preferred_element_type=f32
            )
            wide = term if wide is None else wide + term
        a_op[:, (1 + t) * L:(2 + t) * L] = row_operand(wide)
    run([own], 1, C + tiles)

    def whole_chunk(k):
        run([prepare(row_of(k))], 0, C + tiles)

    def forward(k):
        src = row_of(k)
        return pltpu.make_async_remote_copy(
            src_ref=b_all.at[src], dst_ref=b_all.at[src], send_sem=b_send.at[k + 1],
            recv_sem=b_recv.at[src], device_id=(row_peer[1], col), device_id_type=MESH,
        )

    def step_direct(i, carry):
        k = 2 * i
        row_arrive(k, b_all, b_recv)
        forward(k).start()
        whole_chunk(k)
        return carry

    def step_forwarded(i, carry):
        k = 2 * i + 1
        row_arrive(k, b_all, b_recv)
        whole_chunk(k)
        return carry

    lax.fori_loop(1, R // 2, step_direct, 0)
    lax.fori_loop(0, R // 2 - 2, step_forwarded, 0)
    for k in range(2, R, 2):
        sends.append(forward(k))

    last = []
    for k in (R - 3, R - 1):
        row_arrive(k, b_all, b_recv)
        last.append(prepare(row_of(k)))
    run(last, 1 + tiles, C + tiles)
    for k in range(C - 1, 0, -1):
        sends.append(col_copy(k, acc.at[0:16, slot(k)], part_in, p_send, p_recv))
        sends[-1].start()
    run(last, 0, 1 + tiles)
    for k in range(C):
        cout[k] = acc[:, L + k * Q:L + (k + 1) * Q]
    for k in range(1, C):
        sends.append(col_copy(k, cout.at[k], cin, q_send, q_recv))
        sends[-1].start()

    signal = sig_ref[0]
    d = d_v[...]
    r = r_v[...]
    total = acc[0:16, slot(0)]
    for k in range(1, C):
        col_arrive(k, part_in, p_recv)
        total = total + part_in[col_peer[k]]
    image = signal * total + noise_ref[0] * d

    lane = lax.broadcasted_iota(jnp.int32, (16, 128), 1)
    sub = lax.broadcasted_iota(jnp.int32, (16, 128), 0)
    packed = jnp.zeros((16, 128), f32)
    for q, product in enumerate((r * r, d * image, r * image, image * image)):
        value = jnp.sum(product, axis=1, keepdims=True)
        packed = packed + jnp.where(lane == sub + 16 * q, value, 0.0)
    packed = jnp.sum(packed, axis=0, keepdims=True)

    me = row * C + col
    st[me] = packed

    def sums_copy(r, c, k):
        return pltpu.make_async_remote_copy(
            src_ref=st.at[me], dst_ref=st.at[me], send_sem=s_send.at[k], recv_sem=s_recv.at[me],
            device_id=(r, c), device_id_type=MESH,
        )

    def sums_arrive(r, c, k):
        peer = r * C + c
        pltpu.make_async_remote_copy(
            src_ref=st.at[peer], dst_ref=st.at[peer], send_sem=s_recv.at[peer],
            recv_sem=s_recv.at[peer], device_id=(r, c), device_id_type=MESH,
        ).wait_recv()

    everyone(lambda r, c, k: sums_copy(r, c, k).start())

    fit = cout[0]
    for k in range(1, C):
        col_arrive(k, cin, q_recv)
        fit = fit + cin[col_peer[k]]

    everyone(sums_arrive)
    sums = jnp.broadcast_to(jnp.sum(st[...], axis=0), (16, 128))

    def column(q):
        return jnp.sum(jnp.where(lane == sub + 16 * q, sums, 0.0), axis=1, keepdims=True)

    norm_now, curvature, cross, image_sq = column(0), column(1), column(2), column(3)
    step_len = norm_now / curvature
    norm_next = jnp.maximum(norm_now - 2.0 * (step_len * cross) + step_len * (step_len * image_sq), 0.0)
    r_new = r - step_len * image
    wn_ref[...] = w_v[...] + step_len * d
    rn_ref[...] = r_new
    dn_ref[...] = r_new + (norm_next / norm_now) * d
    cf_ref[...] = prior_v[...] + signal * (fit[16:32] + step_len * fit[0:16])
    for copy in sends:
        copy.wait_send()
    everyone(lambda r, c, k: sums_copy(r, c, k).wait_send())


def hand_over(*refs):
    for i in range(4):
        refs[4 + i][...] = refs[i][...]


def per_device(R, C, points, candidates, length_scales, signal_var, noise_var, cand_prior, weights, residual, direction):
    F, L = points.shape
    Q = candidates.shape[1]
    cols = weights.shape[0]
    tiles = C * Q // L
    hbm = pl.BlockSpec(memory_space=pl.ANY)
    smem = pl.BlockSpec(memory_space=pltpu.SMEM)
    vmem = pl.BlockSpec(memory_space=pltpu.VMEM)
    dma = pltpu.SemaphoreType.DMA
    state = jax.ShapeDtypeStruct((cols, L), f32)
    shapes = (state, state, state, jax.ShapeDtypeStruct((cols, Q), f32))
    results = pl.pallas_call(
        functools.partial(kernel, R, C),
        out_shape=shapes,
        in_specs=[hbm, hbm, hbm, smem, smem, hbm, hbm, hbm, hbm],
        out_specs=(vmem, vmem, vmem, vmem),
        scratch_shapes=[
            pltpu.VMEM((F, L), f32),
            pltpu.VMEM((F, Q), f32),
            pltpu.VMEM((1, F), f32),
            pltpu.VMEM((1, Q), f32),
            pltpu.VMEM((cols, L), f32),
            pltpu.VMEM((cols, L), f32),
            pltpu.VMEM((cols, L), f32),
            pltpu.VMEM((R, F + 2 * cols, L), bf16),
            pltpu.VMEM((C, F, L), bf16),
            pltpu.VMEM((C, F, Q), bf16),
            pltpu.VMEM((128, (C + tiles) * L), bf16),
            pltpu.VMEM((4, L, L), f32),
            pltpu.VMEM((4, L, L), bf16),
            pltpu.VMEM((2 * cols, (C + tiles) * L), f32),
            pltpu.VMEM((C, cols, L), f32),
            pltpu.VMEM((C, 2 * cols, Q), f32),
            pltpu.VMEM((C, 2 * cols, Q), f32),
            pltpu.VMEM((R * C, 1, 128), f32),
            dma((7,)),
            dma((R,)), dma((R,)),
            dma((C,)), dma((C,)),
            dma((C,)), dma((C,)),
            dma((C,)), dma((C,)),
            dma((C,)), dma((C,)),
            dma((R * C,)), dma((R * C,)),
        ],
        compiler_params=pltpu.CompilerParams(
            collective_id=0, has_side_effects=True, vmem_limit_bytes=VMEM_LIMIT
        ),
    )(
        points, candidates, length_scales[None, :], signal_var, noise_var,
        cand_prior[None, :], weights, residual, direction,
    )
    return pl.pallas_call(
        hand_over,
        out_shape=shapes,
        in_specs=[vmem] * 4,
        out_specs=(vmem,) * 4,
        compiler_params=pltpu.CompilerParams(vmem_limit_bytes=VMEM_LIMIT),
    )(*results)


def solution(mesh):
    split = P(None, ("row", "col"))
    return jax.shard_map(
        functools.partial(per_device, mesh.shape["row"], mesh.shape["col"]),
        mesh=mesh,
        in_specs=(split, split, P(), P(), P(), P(("row", "col")), split, split, split),
        out_specs=(split, split, split, split),
        check_vma=False,
    )
```
